128 devices in a mesh: dp: 2 (over core), row: 8 (over x_lo, y), col: 8 (over z, x_hi).
Axes of the slice: x: 4 (x_hi: 2, x_lo: 2; x = x_hi * 2 + x_lo), y: 4, z: 4, core: 2. Of those that a mesh axis runs over, the one named last changes fastest.
Arguments:
- expected: bfloat16 [4096, 8192], P(('dp', 'col'), 'row'), may hold values from -6 to 6
- labels: int32 [4096], replicated, may hold values from 0 to 65535
- unembedding: bfloat16 [65536, 8192], P(('dp', 'col'), 'row'), may hold values from -6 to 6
- down_weight: bfloat16 [28672, 8192], P('col', 'row'), may hold values from -0.0625 to 0.0625
Outputs:
- hidden_grad: bfloat16 [4096, 28672], P(('dp', 'row'), 'col')
- fisher_factor: float32 [8192, 8192], P('row', ('dp', 'col'))
The draws below stay inside these ranges and needn't reach their ends.
All inputs are finite; a program needn't handle non-finite values.
Results may differ from the reference program's by a relative error of at most 0.0051.
Values may be sent and summed in bfloat16 or wider, within the bound.
A program may use at most 256 MiB of HBM per device.

```python
import math
import jax
import jax.numpy as jnp
import numpy as np

D = 8192
FF = 28672
VOCAB = 65536
TOKENS = 4096


def place_ends(entries, key, least, largest):
    longest = entries.shape.index(max(entries.shape))
    spots = []
    for shift in (0, 1):
        where = [jax.random.randint(jax.random.fold_in(key, axis), (), 0, length) for axis, length in enumerate(entries.shape)]
        where[longest] = (where[longest] + shift) % entries.shape[longest]
        spots.append(tuple(where))
    return entries.at[spots[0]].set(least).at[spots[1]].set(largest)


def block_scale(own_key, extent, cuts, smallest, top_value):
    factor_of, own = 1.0, jax.random.fold_in(own_key, 6)
    for position, parts in cuts:
        draws = jnp.exp(jax.random.uniform(jax.random.fold_in(own, position), (parts,), jnp.float32, smallest / len(cuts), top_value / len(cuts)))
        factor_of = factor_of * jnp.repeat(draws, extent[position] // parts).reshape([-1 if axis == position else 1 for axis in range(len(extent))])
    return factor_of


def rank_bounds(number_of, slope):
    loads = [(1 << 20) // math.isqrt(standing ** slope) + 1 for standing in range(1, number_of + 1)]
    deviation = 1 + sum(loads) // (1 << 30)
    return np.cumsum(np.array([max(1, weight // deviation) for weight in loads]))


def ranked_ids(key, dims, number_of, slope):
    grid = rank_bounds(number_of, slope)
    ticket = jax.random.randint(jax.random.fold_in(key, 1), dims, 0, int(grid[number_of - 1]))
    rank = jnp.searchsorted(jnp.asarray(grid, jnp.int32), ticket, side="right")
    return jax.random.permutation(jax.random.fold_in(key, 2), number_of)[rank].astype(jnp.int32)


def centred(own_key, extent, deviation, bound, cuts=(), kind=jnp.bfloat16):
    entries = deviation * jax.random.normal(own_key, extent, jnp.float32)
    if cuts:
        entries = entries * block_scale(own_key, extent, cuts, -0.22, 0.18)
    return jnp.clip(entries, -bound, bound).astype(kind)


def setup_inputs(seed: int = 0) -> dict:
    key_list = jax.random.split(jax.random.key(seed), 5)
    return {
        "expected": centred(key_list[0], (TOKENS, D), 1.0, 6.0, ((0, 16), (1, 8))),
        "labels": place_ends(ranked_ids(key_list[1], (TOKENS,), VOCAB, 2), jax.random.fold_in(key_list[1], 3), 0, VOCAB - 1).astype(jnp.int32),
        "unembedding": centred(key_list[2], (VOCAB, D), 1.0, 6.0, ((0, 16), (1, 8))),
        "down_weight": centred(key_list[3], (FF, D), D ** -0.5, 0.0625, ((0, 8), (1, 8))),
    }


def reference(expected, labels, unembedding, down_weight):
    label_rows = jnp.take(unembedding, labels, axis=0)
    out_grad = (expected.astype(jnp.float32) - label_rows.astype(jnp.float32)).astype(jnp.bfloat16)
    hidden_grad = jnp.dot(out_grad, down_weight.T, preferred_element_type=jnp.float32).astype(jnp.bfloat16)
    fisher_factor = jnp.dot(out_grad.T, out_grad, preferred_element_type=jnp.float32) / TOKENS
    return hidden_grad, fisher_factor
```

```python
import jax
import jax.numpy as jnp
from jax import lax
from jax.experimental import pallas as pl
from jax.experimental.pallas import tpu as pltpu
from jax.sharding import PartitionSpec as P

CAP = 32
EARLY = 3
F_AT = 5
TILE = 256
DEPTH = 512
PART = 128
UNITS = 2 * (TILE // PART)
MESH = pl.DeviceIdType.MESH


def dense_rows(ids, unembedding, place):
    ring = lax.axis_size("dp") * lax.axis_size("col")
    voc_shard = unembedding.shape[0]
    tokens = ids.shape[1]

    def held(k):
        block = lax.rem(place + 2 * ring - 1 - k, ring)
        local = lax.dynamic_slice_in_dim(ids, block, 1, 0).reshape(tokens) - place * voc_shard
        inside = (local >= 0) & (local < voc_shard)
        rows = jnp.take(unembedding, jnp.clip(local, 0, voc_shard - 1), axis=0, mode="clip")
        return jnp.where(inside[:, None], rows, jnp.zeros_like(rows))

    def step(k, total):
        moved = lax.ppermute(total, ("dp", "col"), [(i, (i + 1) % ring) for i in range(ring)])
        return moved + held(k)

    return lax.fori_loop(1, ring, step, held(0))


def dot_nt(x, w):
    return lax.dot_general(x, w, (((1,), (1,)), ((), ())), preferred_element_type=jnp.float32)


def dot_tn(x, w):
    return lax.dot_general(x, w, (((0,), (0,)), ((), ())), preferred_element_type=jnp.float32)


def kernel(
    row_ref, slot_ref, exp_ref, extra_ref, u_ref, w_ref,
    hid_ref, fis_out, f_in,
    u_rest, lab_out, lab_in, grad_own, g_all, g_sib, g_col, c_mid, w_own, w_part,
    tr_out, tr_in, pl_out, pl_in, cb_out, cb_in, own_sum, fis_ref, f_out,
    u_s, lab_ss, lab_rs, wl_s, wd_ss, wd_rs, wf_ss, wf_rs, gx_ss, g_rs, gz_ss,
    tr_ss, tr_rs, pl_ss, pl_rs, cb_ss, cb_rs, sib_ss, sib_rs, cy_ss, cy_rs, col_ss, col_rs, f_ss, f_rs, fis_s,
):
    d = lax.axis_index("dp")
    r = lax.axis_index("row")
    c = lax.axis_index("col")
    a, y = r // 4, r % 4
    z, b = c // 2, c % 2
    v = d * 8 + c
    half = w_ref.shape[0] // 2
    n_chunk = half // TILE
    a_to = z // 2

    def dev(d_, a_, y_, z_, b_):
        return {"dp": d_, "row": a_ * 4 + y_, "col": z_ * 2 + b_}

    def rc(src, dst, ss, rs, to):
        return pltpu.make_async_remote_copy(
            src_ref=src, dst_ref=dst, send_sem=ss, recv_sem=rs, device_id=to, device_id_type=MESH
        )

    def loop(n, body, start=0):
        def step(i, carry):
            body(i)
            return carry

        lax.fori_loop(start, n, step, 0)

    sibling = dev(1 - d, a, y, z, b)
    partner = dev(d, 1 - a, y, z, b)

    bar = pltpu.get_barrier_semaphore()

    def hello(to):
        pl.semaphore_signal(bar, inc=1, device_id=to, device_id_type=MESH)

    def group_dev(k):
        w = lax.rem(v + k, 16)
        return {"dp": w // 8, "row": r, "col": lax.rem(w, 8)}

    loop(16, lambda k: hello(group_dev(k)), 1)
    loop(8, lambda k: hello({"dp": d, "row": (1 - a) * 4 + y, "col": k}))
    up_y = dev(d, a, lax.rem(y + 1, 4), z, b)
    dn_y = dev(d, a, lax.rem(y + 3, 4), z, b)
    hello(up_y)
    hello(dn_y)
    hello(dev(d, a, lax.rem(y + 2, 4), z, b))

    def w_rows(i, h):
        return pl.ds(pl.multiple_of((d if h == 0 else 1 - d) * half + i * TILE, TILE), TILE)

    def wd_copy(i):
        rows = w_rows(i, 0)
        return rc(w_ref.at[rows], w_part.at[rows], wd_ss.at[i], wd_rs.at[i], partner)

    def wf_copy(i):
        rows = w_rows(i, 0)
        return rc(w_part.at[rows], w_part.at[rows], wf_ss.at[i], wf_rs.at[i], sibling)

    def wf_wait(i):
        rows = w_rows(i, 1)
        rc(w_part.at[rows], w_part.at[rows], wf_ss.at[i], wf_rs.at[i], sibling).wait_recv()

    depth = u_rest.shape[0]
    n_deep = u_ref.shape[0] // depth

    def u_load(k):
        src = u_ref.at[pl.ds(pl.multiple_of(k * depth, depth), depth)]
        return pltpu.make_async_copy(src, w_own.at[pl.ds(pl.multiple_of(k * depth, depth), depth)], u_s.at[k])

    u_last = pltpu.make_async_copy(u_ref.at[pl.ds((n_deep - 1) * depth, depth)], u_rest, u_s.at[n_deep - 1])
    loop(n_deep - 1, lambda k: u_load(k).start())
    u_last.start()

    def choose(k, held, fresh):
        rows = held[...]
        for m in range(lab_out.shape[0] // TILE):
            wanted = row_ref[:, m * TILE:(m + 1) * TILE] - k * depth
            pick = jnp.where(
                lax.broadcasted_iota(jnp.int32, (depth, TILE), 0) == wanted, 1.0, 0.0
            ).astype(jnp.bfloat16)
            for n in range(rows.shape[1] // TILE):
                found = dot_tn(pick, rows[:, n * TILE:(n + 1) * TILE])
                own_sum[m, n] = found if fresh else own_sum[m, n] + found

    u_last.wait()
    choose(n_deep - 1, u_rest, True)
    pl.semaphore_wait(bar, 26)

    def choose_next(k):
        u_load(k).wait()
        choose(k, w_own.at[pl.ds(pl.multiple_of(k * depth, depth), depth)], False)

    loop(n_deep - 1, choose_next)
    for m in range(lab_out.shape[0] // TILE):
        for n in range(lab_out.shape[1] // TILE):
            lab_out[m * TILE:(m + 1) * TILE, n * TILE:(n + 1) * TILE] = own_sum[m, n].astype(jnp.bfloat16)
    w_load = pltpu.make_async_copy(w_ref, w_own, wl_s)
    w_load.start()

    width = lab_in.shape[1] // 2

    def side(f):
        return pl.ds(pl.multiple_of(f * width, width), width)

    def lab_copy(k, f):
        w = lax.rem(v + k, 16)
        return rc(
            lab_out.at[pl.ds(pl.multiple_of(w * CAP, CAP), CAP), side(f)],
            lab_in.at[pl.ds(pl.multiple_of(v * CAP, CAP), CAP), side(f)],
            lab_ss.at[f, k], lab_rs.at[f, k], group_dev(k),
        )

    mine = pl.ds(pl.multiple_of(v * CAP, CAP), CAP)
    lab_local = pltpu.make_async_copy(lab_out.at[mine], lab_in.at[mine], lab_rs.at[0, 0])
    lab_local.start()
    for f in range(2):
        loop(16, lambda k: lab_copy(k, f).start(), 1)

    def lab_wait(k, f):
        w = lax.rem(v + 16 - k, 16)
        rows = pl.ds(pl.multiple_of(w * CAP, CAP), CAP)
        rc(
            lab_in.at[rows, side(f)], lab_in.at[rows, side(f)], lab_ss.at[f, k], lab_rs.at[f, k],
            {"dp": w // 8, "row": r, "col": lax.rem(w, 8)},
        ).wait_recv()

    lab_local.wait()
    n_slot = lab_in.shape[0]
    chosen = jnp.where(
        lax.broadcasted_iota(jnp.int32, (n_slot, TILE), 0) == slot_ref[...], 1.0, 0.0
    ).astype(jnp.bfloat16)

    def make_grad(n):
        cols = pl.ds(pl.multiple_of(n * TILE, TILE), TILE)
        rows = dot_tn(chosen, lab_in[:, cols])
        rows = rows + extra_ref[:, cols].astype(jnp.float32)
        grad_own[:, cols] = (exp_ref[:, cols].astype(jnp.float32) - rows).astype(jnp.bfloat16)

    def grad_side(f):
        loop(16, lambda k: lab_wait(k, f), 1)
        loop((f + 1) * (width // TILE), make_grad, f * (width // TILE))

    n_part = TILE // PART
    kk = jnp.where(a == a_to, 0, 1)

    def part_rows(block, s):
        return pl.ds(pl.multiple_of(block * TILE + s * PART, PART), PART)

    def gx_parts(f, s):
        src = grad_own.at[part_rows(0, s), side(f)]
        dst = g_all.at[kk, part_rows(lax.rem(z, 2) * 2 + b, s), side(f)]
        sem = g_rs.at[lax.rem(z, 2) * 4 + b * 2 + kk, f * n_part + s]
        near = rc(src, dst, gx_ss.at[0, f * n_part + s], sem, partner)
        far = rc(src, dst, gx_ss.at[1, f * n_part + s], sem, dev(d, a_to, y, z, 1 - b))
        return near, far, (src, dst, sem)

    def gx_start(f, s):
        near, far, here = gx_parts(f, s)

        @pl.when(a == a_to)
        def _():
            pltpu.make_async_copy(*here).start()

        @pl.when(a != a_to)
        def _():
            near.start()

        far.start()

    zeta = lax.rem(z - 2 * a + 4, 4)
    first = lax.rem((zeta + 1) // 2, 2)
    up_z = dev(d, a, y, lax.rem(z + 1, 4), b)
    dn_z = dev(d, a, y, lax.rem(z + 3, 4), b)

    def g_copy(par, q, f, s, way):
        block = g_all.at[lax.rem(q, 2), part_rows(par * 2 + q // 2, s), side(f)]
        u = f * n_part + s
        return rc(
            block, block, gz_ss.at[way, q, u], g_rs.at[par * 4 + q, u], up_z if way == 0 else dn_z
        )

    def g_order(i):
        return jnp.where(i < 2, b, 1 - b) * 2 + ((i + 1) // 2) % 2

    def unit(t):
        u = lax.rem(t, 2 * UNITS)
        return g_order(t // (2 * UNITS) * 2 + lax.rem(u // n_part, 2)), u // UNITS, lax.rem(u, n_part)

    def relay(t):
        q, f, s = unit(t)
        g_copy(first, q, f, s, 0).wait_recv()

        @pl.when(zeta != 3)
        def _():
            g_copy(first, q, f, s, 0).start()

        @pl.when(zeta != 2)
        def _():
            g_copy(first, q, f, s, 1).start()

    grad_side(0)
    loop(n_part, lambda s: gx_start(0, s))

    @pl.when(zeta < 2)
    def _():
        loop(n_part, relay)

    grad_side(1)
    loop(n_part, lambda s: gx_start(1, s))
    loop(n_chunk, lambda i: wd_copy(i).start())

    def partial(y_, i, h):
        rows = pl.ds(pl.multiple_of(y_ * TILE, TILE), TILE)
        wr = w_rows(i, h)
        return dot_nt(g_all[0, rows, :], w_own[wr, :]) + dot_nt(g_all[1, rows, :], w_part[wr, :])

    def ahead(h):
        return up_y if h == 0 else dn_y

    def behind(h):
        return dn_y if h == 0 else up_y

    def y_off(h, n):
        return lax.rem(y + (n if h == 0 else 4 - n), 4)

    def tr_copy(i, h):
        return rc(tr_out.at[h, i], tr_in.at[h, i], tr_ss.at[h, i], tr_rs.at[h, i], ahead(h))

    def pl_copy(i, h):
        return rc(pl_out.at[h, i], pl_in.at[h, i], pl_ss.at[h, i], pl_rs.at[h, i], behind(h))

    def cb_copy(i, h):
        return rc(cb_out.at[h, i], cb_in.at[h, i], cb_ss.at[h, i], cb_rs.at[h, i], ahead(h))

    def transit(i, h):
        tr_out[h, i] = partial(y_off(h, 2), i, h).astype(jnp.bfloat16)
        tr_copy(i, h).start()

    def plain(i, h):
        pl_out[h, i] = partial(y_off(h, 3), i, h).astype(jnp.bfloat16)
        pl_copy(i, h).start()

    def keep(i, h):
        own_sum[h, i] = partial(y, i, h)

    def combine(i, h):
        part = partial(y_off(h, 1), i, h)
        tr_copy(i, h).wait_recv()
        cb_out[h, i] = (part + tr_in[h, i].astype(jnp.float32)).astype(jnp.bfloat16)
        cb_copy(i, h).start()


    def col_row(zeta_):
        near = lax.rem((zeta_ + 1) // 2, 2)
        side = jnp.where(zeta_ < 2, 1 - b, b)
        return pl.ds(pl.multiple_of((near * 2 + side) * TILE, TILE), TILE)

    z_row = col_row(zeta)
    b_cols = side(b)

    def cy_copy(n, d_):
        src = g_all.at[jnp.where(d_ == a, 0, 1), z_row, b_cols]
        return rc(src, c_mid.at[n - 1, d_], cy_ss.at[n - 1, d_], cy_rs.at[n - 1, d_],
                  dev(d, a, lax.rem(y + n, 4), z, b))

    def cy_each(act):
        def step(k):
            act(cy_copy(k // 2 + 1, lax.rem(k, 2)))

        loop(6, step)

    @pl.when(zeta >= 2)
    def _():
        loop(2 * UNITS, relay)
        cy_each(lambda copy: copy.start())

    @pl.when(zeta < 2)
    def _():
        loop(4 * UNITS, relay, n_part)
        cy_each(lambda copy: copy.start())

    def second_wait(t):
        g_copy(1 - first, *unit(t), 0).wait_recv()

    loop(2 * UNITS, second_wait)
    w_load.wait()
    even = lax.rem(y, 2) == b

    def early_step(i):
        wd_copy(i).wait_recv()
        wf_copy(i).start()
        for h in range(2):
            if h == 1:
                wf_wait(i)

            @pl.when(even)
            def _():
                transit(i, h)
                keep(i, h)

            @pl.when(jnp.logical_not(even))
            def _():
                plain(i, h)

                @pl.when(i > 0)
                def _():
                    combine(i - 1, h)

        @pl.when(jnp.logical_and(zeta >= 2, i < 2))
        def _():
            loop((3 + i) * UNITS, relay, (2 + i) * UNITS)

    loop(EARLY, early_step)
    loop(4 * UNITS, second_wait, 2 * UNITS)
    sib_copy = rc(g_all, g_sib, sib_ss, sib_rs, sibling)
    sib_copy.start()

    def cz_parts(k):
        n, d_ = k // 2, lax.rem(k, 2)
        z_to = lax.rem(y + 4 - n, 4)
        dst = g_col.at[d, z_row]
        sem = col_rs.at[d * 4 + zeta]
        mid = c_mid.at[jnp.maximum(n - 1, 0), d_]
        own = g_all.at[jnp.where(d_ == a, 0, 1), z_row, b_cols]
        is_self = jnp.logical_and(z_to == z, d_ == d)
        to = dev(d_, a, y, z_to, b)
        return n, is_self, mid, own, dst, sem, to

    def cz_start(k):
        n, is_self, mid, own, dst, sem, to = cz_parts(k)
        for src, has in ((own, n == 0), (mid, n > 0)):
            @pl.when(jnp.logical_and(has, is_self))
            def _():
                pltpu.make_async_copy(src, dst, sem).start()

            @pl.when(jnp.logical_and(has, jnp.logical_not(is_self)))
            def _():
                rc(src, dst, col_ss.at[k], sem, to).start()

    cy_each(lambda copy: copy.wait_recv())
    loop(8, cz_start)

    lag = 1

    @pl.when(jnp.logical_not(even))
    def _():
        for h in range(2):
            combine(EARLY - 1, h)

    def other_step(i):
        for h in range(2):

            @pl.when(even)
            def _():
                plain(i, h)

            @pl.when(jnp.logical_not(even))
            def _():
                transit(i, h)
                keep(i, h)

    loop(EARLY, other_step)

    def hidden_step(i):
        wd_copy(i).wait_recv()
        wf_copy(i).start()
        for h in range(2):
            if h == 1:
                wf_wait(i)
            transit(i, h)
            plain(i, h)
            keep(i, h)

        @pl.when(jnp.logical_and(even, i < 2 * EARLY))
        def _():
            for h in range(2):
                combine(i - EARLY, h)

        @pl.when(i >= EARLY + lag)
        def _():
            for h in range(2):
                combine(i - lag, h)

    loop(F_AT, hidden_step, EARLY)

    def col_wait(k):
        d_, z_ = k // 4, lax.rem(k, 4)
        block = g_col.at[d_, col_row(z_)]
        rc(block, block, col_ss.at[k], col_rs.at[k], sibling).wait_recv()

    loop(8, col_wait)
    sib_copy.wait_recv()
    n_feat = g_all.shape[2] // TILE

    def fisher_part(k, n):
        cols = pl.ds(pl.multiple_of(n * TILE, TILE), TILE)
        return dot_tn(g_all[k, :, cols], g_col[d]) + dot_tn(g_sib[k, :, cols], g_col[1 - d])

    f_copy = rc(f_out, f_in, f_ss, f_rs, partner)

    def fisher_other(n):
        f_out[pl.ds(pl.multiple_of(n * TILE, TILE), TILE), :] = fisher_part(1, n).astype(jnp.bfloat16)

    loop(n_feat, fisher_other)
    f_copy.start()

    loop(n_chunk, hidden_step, F_AT)

    def late_step(i):
        for h in range(2):
            combine(i, h)

    loop(n_chunk, late_step, n_chunk - lag)

    def fisher_own(n):
        fis_ref[pl.ds(pl.multiple_of(n * TILE, TILE), TILE), :] = fisher_part(0, n)

    loop(n_feat, fisher_own)
    fis_copy = pltpu.make_async_copy(fis_ref, fis_out, fis_s)
    fis_copy.start()

    def hidden_out(i):
        for h in range(2):
            pl_copy(i, h).wait_recv()
            cb_copy(i, h).wait_recv()
            total = own_sum[h, i] + pl_in[h, i].astype(jnp.float32) + cb_in[h, i].astype(jnp.float32)
            hid_ref[:, w_rows(i, h)] = total.astype(jnp.bfloat16)

    loop(n_chunk, hidden_out)
    f_copy.wait_recv()
    fis_copy.wait()

    for f in range(2):
        loop(16, lambda k: lab_copy(k, f).wait_send(), 1)

    def gx_done(f, s):
        near, far, _ = gx_parts(f, s)

        @pl.when(a != a_to)
        def _():
            near.wait_send()

        far.wait_send()

    for f in range(2):
        loop(n_part, lambda s: gx_done(f, s))

    def relay_done(t):
        q, f, s = unit(t)

        @pl.when(zeta != 3)
        def _():
            g_copy(first, q, f, s, 0).wait_send()

        @pl.when(zeta != 2)
        def _():
            g_copy(first, q, f, s, 1).wait_send()

    loop(4 * UNITS, relay_done)
    sib_copy.wait_send()

    def cz_done(k):
        n, is_self, mid, own, dst, sem, to = cz_parts(k)

        @pl.when(jnp.logical_not(is_self))
        def _():
            rc(mid, dst, col_ss.at[k], sem, to).wait_send()

    loop(8, cz_done)
    cy_each(lambda copy: copy.wait_send())

    def rest_done(i):
        wd_copy(i).wait_send()
        wf_copy(i).wait_send()
        for h in range(2):
            tr_copy(i, h).wait_send()
            pl_copy(i, h).wait_send()
            cb_copy(i, h).wait_send()

    loop(n_chunk, rest_done)
    f_copy.wait_send()


def fast_shards(expected, extra, row_ids, slots, unembedding, down_weight):
    tokens, feats = expected.shape
    hidden = down_weight.shape[0]
    n_chunk = hidden // 2 // TILE
    bf16, f32 = jnp.bfloat16, jnp.float32
    total_tokens = tokens * 16
    vmem, dma = pltpu.VMEM, pltpu.SemaphoreType.DMA
    chunks = (2, n_chunk, TILE, TILE)
    any_spec = pl.BlockSpec(memory_space=pl.ANY)
    vmem_spec = pl.BlockSpec(memory_space=pltpu.VMEM)
    hidden_grad, own, other = pl.pallas_call(
        kernel,
        out_shape=(
            jax.ShapeDtypeStruct((tokens, hidden), bf16),
            jax.ShapeDtypeStruct((feats, feats // 2), f32),
            jax.ShapeDtypeStruct((feats, feats // 2), bf16),
        ),
        in_specs=[vmem_spec] * 4 + [any_spec] * 2,
        out_specs=(vmem_spec, any_spec, any_spec),
        scratch_shapes=[
            vmem((DEPTH, feats), bf16),
            vmem((16 * CAP, feats), bf16),
            vmem((16 * CAP, feats), bf16),
            vmem((tokens, feats), bf16),
            vmem((2, 4 * tokens, feats), bf16),
            vmem((2, 4 * tokens, feats), bf16),
            vmem((2, 4 * tokens, feats // 2), bf16),
            vmem((3, 2, tokens, feats // 2), bf16),
            vmem((hidden, feats), bf16),
            vmem((hidden, feats), bf16),
            vmem(chunks, bf16), vmem(chunks, bf16),
            vmem(chunks, bf16), vmem(chunks, bf16),
            vmem(chunks, bf16), vmem(chunks, bf16),
            vmem(chunks, f32),
            vmem((feats, feats // 2), f32),
            vmem((feats, feats // 2), bf16),
            dma((unembedding.shape[0] // DEPTH,)), dma((2, 16)), dma((2, 16)), dma,
            dma((n_chunk,)), dma((n_chunk,)), dma((n_chunk,)), dma((n_chunk,)),
            dma((2, UNITS)), dma((8, UNITS)), dma((2, 4, UNITS)),
            dma((2, n_chunk)), dma((2, n_chunk)), dma((2, n_chunk)),
            dma((2, n_chunk)), dma((2, n_chunk)), dma((2, n_chunk)),
            dma, dma, dma((3, 2)), dma((3, 2)), dma((8,)), dma((8,)), dma, dma, dma,
        ],
        compiler_params=pltpu.CompilerParams(
            collective_id=0, has_side_effects=True, vmem_limit_bytes=60 * 1024 * 1024
        ),
    )(row_ids, slots, expected, extra, unembedding, down_weight)
    return hidden_grad, (own + other.astype(f32)) / total_tokens


def shards(expected, labels, unembedding, down_weight):
    tokens = expected.shape[0]
    voc_shard = unembedding.shape[0]
    place = lax.axis_index("dp") * lax.axis_size("col") + lax.axis_index("col")
    ids = labels.reshape(-1, tokens)
    owner = ids // voc_shard
    before = lax.broadcasted_iota(jnp.int32, (1, tokens, tokens), 1) > lax.broadcasted_iota(
        jnp.int32, (1, tokens, tokens), 2
    )
    same_label = ids[:, :, None] == ids[:, None, :]
    is_first = jnp.logical_not(jnp.any(same_label & before, axis=2))
    ahead = (owner[:, :, None] == owner[:, None, :]) & before & is_first[:, None, :]
    rank = jnp.sum(ahead.astype(jnp.int32), axis=2)
    fits = jnp.max(jnp.where(is_first, rank, 0)) < CAP
    at_slot = ((owner == place) & is_first)[:, None, :] & (
        rank[:, None, :] == lax.broadcasted_iota(jnp.int32, (1, CAP, 1), 1)
    )
    row_ids = jnp.sum(jnp.where(at_slot, (ids - place * voc_shard)[:, None, :], 0), axis=2).reshape(1, -1)

    def mine(x):
        return lax.dynamic_slice_in_dim(x, place, 1, 0)

    own_ids = mine(ids)
    holds = (own_ids.reshape(tokens, 1) == own_ids) & mine(is_first).reshape(tokens, 1)
    slots = jnp.sum(jnp.where(holds, mine(owner * CAP + rank).reshape(tokens, 1), 0), axis=0, keepdims=True)
    extra = lax.cond(
        fits,
        lambda: jnp.zeros_like(expected),
        lambda: dense_rows(ids, unembedding, place),
    )
    slots = jnp.where(fits, slots, -1)
    return fast_shards(expected, extra, row_ids, slots, unembedding, down_weight)


def solution(mesh):
    in_specs = (P(("dp", "col"), "row"), P(), P(("dp", "col"), "row"), P("col", "row"))
    out_specs = (P(("dp", "row"), "col"), P("row", ("dp", "col")))
    return jax.shard_map(shards, mesh=mesh, in_specs=in_specs, out_specs=out_specs, check_vma=False)
```

```python
import jax
import jax.numpy as jnp
from jax import lax
from jax.experimental import pallas as pl
from jax.experimental.pallas import tpu as pltpu
from jax.sharding import PartitionSpec as P

CAP = 32
EARLY = 3
F_AT = 5
TILE = 256
DEPTH = 512
PART = 128
UNITS = 2 * (TILE // PART)
MESH = pl.DeviceIdType.MESH


def dense_rows(ids, unembedding, place):
    ring = lax.axis_size("dp") * lax.axis_size("col")
    voc_shard = unembedding.shape[0]
    tokens = ids.shape[1]

    def held(k):
        block = lax.rem(place + 2 * ring - 1 - k, ring)
        local = lax.dynamic_slice_in_dim(ids, block, 1, 0).reshape(tokens) - place * voc_shard
        inside = (local >= 0) & (local < voc_shard)
        rows = jnp.take(unembedding, jnp.clip(local, 0, voc_shard - 1), axis=0, mode="clip")
        return jnp.where(inside[:, None], rows, jnp.zeros_like(rows))

    def step(k, total):
        moved = lax.ppermute(total, ("dp", "col"), [(i, (i + 1) % ring) for i in range(ring)])
        return moved + held(k)

    return lax.fori_loop(1, ring, step, held(0))


def dot_nt(x, w):
    return lax.dot_general(x, w, (((1,), (1,)), ((), ())), preferred_element_type=jnp.float32)


def dot_tn(x, w):
    return lax.dot_general(x, w, (((0,), (0,)), ((), ())), preferred_element_type=jnp.float32)


def kernel(
    row_ref, slot_ref, exp_ref, extra_ref, u_ref, w_ref,
    hid_ref, fis_out, f_in,
    u_rest, lab_out, lab_in, grad_own, g_all, g_sib, g_col, c_mid, w_own, w_part,
    tr_out, tr_in, pl_out, pl_in, cb_out, cb_in, own_sum, fis_ref, f_out,
    u_s, lab_ss, lab_rs, wl_s, wd_ss, wd_rs, wf_ss, wf_rs, gx_ss, g_rs, gz_ss,
    tr_ss, tr_rs, pl_ss, pl_rs, cb_ss, cb_rs, sib_ss, sib_rs, cy_ss, cy_rs, col_ss, col_rs, f_ss, f_rs, fis_s,
):
    d = lax.axis_index("dp")
    r = lax.axis_index("row")
    c = lax.axis_index("col")
    a, y = r // 4, r % 4
    z, b = c // 2, c % 2
    v = d * 8 + c
    half = w_ref.shape[0] // 2
    n_chunk = half // TILE
    a_to = z // 2

    def dev(d_, a_, y_, z_, b_):
        return {"dp": d_, "row": a_ * 4 + y_, "col": z_ * 2 + b_}

    def rc(src, dst, ss, rs, to):
        return pltpu.make_async_remote_copy(
            src_ref=src, dst_ref=dst, send_sem=ss, recv_sem=rs, device_id=to, device_id_type=MESH
        )

    def loop(n, body, start=0):
        def step(i, carry):
            body(i)
            return carry

        lax.fori_loop(start, n, step, 0)

    sibling = dev(1 - d, a, y, z, b)
    partner = dev(d, 1 - a, y, z, b)

    bar = pltpu.get_barrier_semaphore()

    def hello(to):
        pl.semaphore_signal(bar, inc=1, device_id=to, device_id_type=MESH)

    def group_dev(k):
        w = lax.rem(v + k, 16)
        return {"dp": w // 8, "row": r, "col": lax.rem(w, 8)}

    loop(16, lambda k: hello(group_dev(k)), 1)
    loop(8, lambda k: hello({"dp": d, "row": (1 - a) * 4 + y, "col": k}))
    up_y = dev(d, a, lax.rem(y + 1, 4), z, b)
    dn_y = dev(d, a, lax.rem(y + 3, 4), z, b)
    hello(up_y)
    hello(dn_y)
    hello(dev(d, a, lax.rem(y + 2, 4), z, b))

    def w_rows(i, h):
        return pl.ds(pl.multiple_of((d if h == 0 else 1 - d) * half + i * TILE, TILE), TILE)

    def wd_copy(i):
        rows = w_rows(i, 0)
        return rc(w_ref.at[rows], w_part.at[rows], wd_ss.at[i], wd_rs.at[i], partner)

    def wf_copy(i):
        rows = w_rows(i, 0)
        return rc(w_part.at[rows], w_part.at[rows], wf_ss.at[i], wf_rs.at[i], sibling)

    def wf_wait(i):
        rows = w_rows(i, 1)
        rc(w_part.at[rows], w_part.at[rows], wf_ss.at[i], wf_rs.at[i], sibling).wait_recv()

    depth = u_rest.shape[0]
    n_deep = u_ref.shape[0] // depth

    def u_load(k):
        src = u_ref.at[pl.ds(pl.multiple_of(k * depth, depth), depth)]
        return pltpu.make_async_copy(src, w_own.at[pl.ds(pl.multiple_of(k * depth, depth), depth)], u_s.at[k])

    u_last = pltpu.make_async_copy(u_ref.at[pl.ds((n_deep - 1) * depth, depth)], u_rest, u_s.at[n_deep - 1])
    loop(n_deep - 1, lambda k: u_load(k).start())
    u_last.start()

    def choose(k, held, fresh):
        rows = held[...]
        for m in range(lab_out.shape[0] // TILE):
            wanted = row_ref[:, m * TILE:(m + 1) * TILE] - k * depth
            pick = jnp.where(
                lax.broadcasted_iota(jnp.int32, (depth, TILE), 0) == wanted, 1.0, 0.0
            ).astype(jnp.bfloat16)
            for n in range(rows.shape[1] // TILE):
                found = dot_tn(pick, rows[:, n * TILE:(n + 1) * TILE])
                own_sum[m, n] = found if fresh else own_sum[m, n] + found

    u_last.wait()
    choose(n_deep - 1, u_rest, True)
    pl.semaphore_wait(bar, 26)

    def choose_next(k):
        u_load(k).wait()
        choose(k, w_own.at[pl.ds(pl.multiple_of(k * depth, depth), depth)], False)

    loop(n_deep - 1, choose_next)
    for m in range(lab_out.shape[0] // TILE):
        for n in range(lab_out.shape[1] // TILE):
            lab_out[m * TILE:(m + 1) * TILE, n * TILE:(n + 1) * TILE] = own_sum[m, n].astype(jnp.bfloat16)
    w_load = pltpu.make_async_copy(w_ref, w_own, wl_s)
    w_load.start()

    width = lab_in.shape[1] // 2

    def side(f):
        return pl.ds(pl.multiple_of(f * width, width), width)

    def lab_copy(k, f):
        w = lax.rem(v + k, 16)
        return rc(
            lab_out.at[pl.ds(pl.multiple_of(w * CAP, CAP), CAP), side(f)],
            lab_in.at[pl.ds(pl.multiple_of(v * CAP, CAP), CAP), side(f)],
            lab_ss.at[f, k], lab_rs.at[f, k], group_dev(k),
        )

    mine = pl.ds(pl.multiple_of(v * CAP, CAP), CAP)
    lab_local = pltpu.make_async_copy(lab_out.at[mine], lab_in.at[mine], lab_rs.at[0, 0])
    lab_local.start()
    for f in range(2):
        loop(16, lambda k: lab_copy(k, f).start(), 1)

    def lab_wait(k, f):
        w = lax.rem(v + 16 - k, 16)
        rows = pl.ds(pl.multiple_of(w * CAP, CAP), CAP)
        rc(
            lab_in.at[rows, side(f)], lab_in.at[rows, side(f)], lab_ss.at[f, k], lab_rs.at[f, k],
            {"dp": w // 8, "row": r, "col": lax.rem(w, 8)},
        ).wait_recv()

    lab_local.wait()
    n_slot = lab_in.shape[0]
    chosen = jnp.where(
        lax.broadcasted_iota(jnp.int32, (n_slot, TILE), 0) == slot_ref[...], 1.0, 0.0
    ).astype(jnp.bfloat16)

    def make_grad(n):
        cols = pl.ds(pl.multiple_of(n * TILE, TILE), TILE)
        rows = dot_tn(chosen, lab_in[:, cols])
        rows = rows + extra_ref[:, cols].astype(jnp.float32)
        grad_own[:, cols] = (exp_ref[:, cols].astype(jnp.float32) - rows).astype(jnp.bfloat16)

    def grad_side(f):
        loop(16, lambda k: lab_wait(k, f), 1)
        loop((f + 1) * (width // TILE), make_grad, f * (width // TILE))

    n_part = TILE // PART
    kk = jnp.where(a == a_to, 0, 1)

    def part_rows(block, s):
        return pl.ds(pl.multiple_of(block * TILE + s * PART, PART), PART)

    def gx_parts(f, s):
        src = grad_own.at[part_rows(0, s), side(f)]
        dst = g_all.at[kk, part_rows(lax.rem(z, 2) * 2 + b, s), side(f)]
        sem = g_rs.at[lax.rem(z, 2) * 4 + b * 2 + kk, f * n_part + s]
        near = rc(src, dst, gx_ss.at[0, f * n_part + s], sem, partner)
        far = rc(src, dst, gx_ss.at[1, f * n_part + s], sem, dev(d, a_to, y, z, 1 - b))
        return near, far, (src, dst, sem)

    def gx_start(f, s):
        near, far, here = gx_parts(f, s)

        @pl.when(a == a_to)
        def _():
            pltpu.make_async_copy(*here).start()

        @pl.when(a != a_to)
        def _():
            near.start()

        far.start()

    zeta = lax.rem(z - 2 * a + 4, 4)
    first = lax.rem((zeta + 1) // 2, 2)
    up_z = dev(d, a, y, lax.rem(z + 1, 4), b)
    dn_z = dev(d, a, y, lax.rem(z + 3, 4), b)

    def g_copy(par, q, f, s, way):
        block = g_all.at[lax.rem(q, 2), part_rows(par * 2 + q // 2, s), side(f)]
        u = f * n_part + s
        return rc(
            block, block, gz_ss.at[way, q, u], g_rs.at[par * 4 + q, u], up_z if way == 0 else dn_z
        )

    def g_order(i):
        return jnp.where(i < 2, b, 1 - b) * 2 + ((i + 1) // 2) % 2

    def unit(t):
        u = lax.rem(t, 2 * UNITS)
        return g_order(t // (2 * UNITS) * 2 + lax.rem(u // n_part, 2)), u // UNITS, lax.rem(u, n_part)

    def relay(t):
        q, f, s = unit(t)
        g_copy(first, q, f, s, 0).wait_recv()

        @pl.when(zeta != 3)
        def _():
            g_copy(first, q, f, s, 0).start()

        @pl.when(zeta != 2)
        def _():
            g_copy(first, q, f, s, 1).start()

    grad_side(0)
    loop(n_part, lambda s: gx_start(0, s))

    @pl.when(zeta < 2)
    def _():
        loop(n_part, relay)

    grad_side(1)
    loop(n_part, lambda s: gx_start(1, s))
    loop(n_chunk, lambda i: wd_copy(i).start())

    def partial(y_, i, h):
        rows = pl.ds(pl.multiple_of(y_ * TILE, TILE), TILE)
        wr = w_rows(i, h)
        return dot_nt(g_all[0, rows, :], w_own[wr, :]) + dot_nt(g_all[1, rows, :], w_part[wr, :])

    def ahead(h):
        return up_y if h == 0 else dn_y

    def behind(h):
        return dn_y if h == 0 else up_y

    def y_off(h, n):
        return lax.rem(y + (n if h == 0 else 4 - n), 4)

    def tr_copy(i, h):
        return rc(tr_out.at[h, i], tr_in.at[h, i], tr_ss.at[h, i], tr_rs.at[h, i], ahead(h))

    def pl_copy(i, h):
        return rc(pl_out.at[h, i], pl_in.at[h, i], pl_ss.at[h, i], pl_rs.at[h, i], behind(h))

    def cb_copy(i, h):
        return rc(cb_out.at[h, i], cb_in.at[h, i], cb_ss.at[h, i], cb_rs.at[h, i], ahead(h))

    def transit(i, h):
        tr_out[h, i] = partial(y_off(h, 2), i, h).astype(jnp.bfloat16)
        tr_copy(i, h).start()

    def plain(i, h):
        pl_out[h, i] = partial(y_off(h, 3), i, h).astype(jnp.bfloat16)
        pl_copy(i, h).start()

    def keep(i, h):
        own_sum[h, i] = partial(y, i, h)

    def combine(i, h):
        part = partial(y_off(h, 1), i, h)
        tr_copy(i, h).wait_recv()
        cb_out[h, i] = (part + tr_in[h, i].astype(jnp.float32)).astype(jnp.bfloat16)
        cb_copy(i, h).start()


    def col_row(zeta_):
        near = lax.rem((zeta_ + 1) // 2, 2)
        side = jnp.where(zeta_ < 2, 1 - b, b)
        return pl.ds(pl.multiple_of((near * 2 + side) * TILE, TILE), TILE)

    z_row = col_row(zeta)
    b_cols = side(b)

    def cy_copy(n, d_):
        src = g_all.at[jnp.where(d_ == a, 0, 1), z_row, b_cols]
        return rc(src, c_mid.at[n - 1, d_], cy_ss.at[n - 1, d_], cy_rs.at[n - 1, d_],
                  dev(d, a, lax.rem(y + n, 4), z, b))

    def cy_each(act):
        def step(k):
            act(cy_copy(k // 2 + 1, lax.rem(k, 2)))

        loop(6, step)

    @pl.when(zeta >= 2)
    def _():
        loop(2 * UNITS, relay)
        cy_each(lambda copy: copy.start())

    @pl.when(zeta < 2)
    def _():
        loop(4 * UNITS, relay, n_part)
        cy_each(lambda copy: copy.start())

    def second_wait(t):
        g_copy(1 - first, *unit(t), 0).wait_recv()

    loop(2 * UNITS, second_wait)
    w_load.wait()
    even = lax.rem(y, 2) == b

    def early_step(i):
        wd_copy(i).wait_recv()
        wf_copy(i).start()
        for h in range(2):
            if h == 1:
                wf_wait(i)

            @pl.when(even)
            def _():
                transit(i, h)
                keep(i, h)

            @pl.when(jnp.logical_not(even))
            def _():
                plain(i, h)

                @pl.when(i > 0)
                def _():
                    combine(i - 1, h)

        @pl.when(jnp.logical_and(zeta >= 2, i < 2))
        def _():
            loop((3 + i) * UNITS, relay, (2 + i) * UNITS)

    loop(EARLY, early_step)

    def cz_parts(k):
        n, d_ = k // 2, lax.rem(k, 2)
        z_to = lax.rem(y + 4 - n, 4)
        dst = g_col.at[d, z_row]
        sem = col_rs.at[d * 4 + zeta]
        mid = c_mid.at[jnp.maximum(n - 1, 0), d_]
        own = g_all.at[jnp.where(d_ == a, 0, 1), z_row, b_cols]
        is_self = jnp.logical_and(z_to == z, d_ == d)
        to = dev(d_, a, y, z_to, b)
        return n, is_self, mid, own, dst, sem, to

    def cz_start(k):
        n, is_self, mid, own, dst, sem, to = cz_parts(k)
        for src, has in ((own, n == 0), (mid, n > 0)):
            @pl.when(jnp.logical_and(has, is_self))
            def _():
                pltpu.make_async_copy(src, dst, sem).start()

            @pl.when(jnp.logical_and(has, jnp.logical_not(is_self)))
            def _():
                rc(src, dst, col_ss.at[k], sem, to).start()

    loop(2, cz_start)
    loop(4 * UNITS, second_wait, 2 * UNITS)
    sib_copy = rc(g_all, g_sib, sib_ss, sib_rs, sibling)
    sib_copy.start()

    def cz_pass(i):
        n = jnp.where(i == 2, 2, 1 + 2 * i)
        for d_ in range(2):
            cy_copy(n, d_).wait_recv()
            cz_start(2 * n + d_)

    loop(3, cz_pass)

    lag = 1

    @pl.when(jnp.logical_not(even))
    def _():
        for h in range(2):
            combine(EARLY - 1, h)

    def other_step(i):
        for h in range(2):

            @pl.when(even)
            def _():
                plain(i, h)

            @pl.when(jnp.logical_not(even))
            def _():
                transit(i, h)
                keep(i, h)

    loop(EARLY, other_step)

    def hidden_step(i):
        wd_copy(i).wait_recv()
        wf_copy(i).start()
        for h in range(2):
            if h == 1:
                wf_wait(i)
            transit(i, h)
            plain(i, h)
            keep(i, h)

        @pl.when(jnp.logical_and(even, i < 2 * EARLY))
        def _():
            for h in range(2):
                combine(i - EARLY, h)

        @pl.when(i >= EARLY + lag)
        def _():
            for h in range(2):
                combine(i - lag, h)

    loop(F_AT, hidden_step, EARLY)

    def col_wait(k):
        d_, z_ = k // 4, lax.rem(k, 4)
        block = g_col.at[d_, col_row(z_)]
        rc(block, block, col_ss.at[k], col_rs.at[k], sibling).wait_recv()

    loop(8, col_wait)
    sib_copy.wait_recv()
    n_feat = g_all.shape[2] // TILE

    def fisher_part(k, n):
        cols = pl.ds(pl.multiple_of(n * TILE, TILE), TILE)
        return dot_tn(g_all[k, :, cols], g_col[d]) + dot_tn(g_sib[k, :, cols], g_col[1 - d])

    f_copy = rc(f_out, f_in, f_ss, f_rs, partner)

    def fisher_other(n):
        f_out[pl.ds(pl.multiple_of(n * TILE, TILE), TILE), :] = fisher_part(1, n).astype(jnp.bfloat16)

    loop(n_feat, fisher_other)
    f_copy.start()

    loop(n_chunk, hidden_step, F_AT)

    def late_step(i):
        for h in range(2):
            combine(i, h)

    loop(n_chunk, late_step, n_chunk - lag)

    def fisher_own(n):
        fis_ref[pl.ds(pl.multiple_of(n * TILE, TILE), TILE), :] = fisher_part(0, n)

    loop(n_feat, fisher_own)
    fis_copy = pltpu.make_async_copy(fis_ref, fis_out, fis_s)
    fis_copy.start()

    def hidden_out(i):
        for h in range(2):
            pl_copy(i, h).wait_recv()
            cb_copy(i, h).wait_recv()
            total = own_sum[h, i] + pl_in[h, i].astype(jnp.float32) + cb_in[h, i].astype(jnp.float32)
            hid_ref[:, w_rows(i, h)] = total.astype(jnp.bfloat16)

    loop(n_chunk, hidden_out)
    f_copy.wait_recv()
    fis_copy.wait()

    for f in range(2):
        loop(16, lambda k: lab_copy(k, f).wait_send(), 1)

    def gx_done(f, s):
        near, far, _ = gx_parts(f, s)

        @pl.when(a != a_to)
        def _():
            near.wait_send()

        far.wait_send()

    for f in range(2):
        loop(n_part, lambda s: gx_done(f, s))

    def relay_done(t):
        q, f, s = unit(t)

        @pl.when(zeta != 3)
        def _():
            g_copy(first, q, f, s, 0).wait_send()

        @pl.when(zeta != 2)
        def _():
            g_copy(first, q, f, s, 1).wait_send()

    loop(4 * UNITS, relay_done)
    sib_copy.wait_send()

    def cz_done(k):
        n, is_self, mid, own, dst, sem, to = cz_parts(k)

        @pl.when(jnp.logical_not(is_self))
        def _():
            rc(mid, dst, col_ss.at[k], sem, to).wait_send()

    loop(8, cz_done)
    cy_each(lambda copy: copy.wait_send())

    def rest_done(i):
        wd_copy(i).wait_send()
        wf_copy(i).wait_send()
        for h in range(2):
            tr_copy(i, h).wait_send()
            pl_copy(i, h).wait_send()
            cb_copy(i, h).wait_send()

    loop(n_chunk, rest_done)
    f_copy.wait_send()


def fast_shards(expected, extra, row_ids, slots, unembedding, down_weight):
    tokens, feats = expected.shape
    hidden = down_weight.shape[0]
    n_chunk = hidden // 2 // TILE
    bf16, f32 = jnp.bfloat16, jnp.float32
    total_tokens = tokens * 16
    vmem, dma = pltpu.VMEM, pltpu.SemaphoreType.DMA
    chunks = (2, n_chunk, TILE, TILE)
    any_spec = pl.BlockSpec(memory_space=pl.ANY)
    vmem_spec = pl.BlockSpec(memory_space=pltpu.VMEM)
    hidden_grad, own, other = pl.pallas_call(
        kernel,
        out_shape=(
            jax.ShapeDtypeStruct((tokens, hidden), bf16),
            jax.ShapeDtypeStruct((feats, feats // 2), f32),
            jax.ShapeDtypeStruct((feats, feats // 2), bf16),
        ),
        in_specs=[vmem_spec] * 4 + [any_spec] * 2,
        out_specs=(vmem_spec, any_spec, any_spec),
        scratch_shapes=[
            vmem((DEPTH, feats), bf16),
            vmem((16 * CAP, feats), bf16),
            vmem((16 * CAP, feats), bf16),
            vmem((tokens, feats), bf16),
            vmem((2, 4 * tokens, feats), bf16),
            vmem((2, 4 * tokens, feats), bf16),
            vmem((2, 4 * tokens, feats // 2), bf16),
            vmem((3, 2, tokens, feats // 2), bf16),
            vmem((hidden, feats), bf16),
            vmem((hidden, feats), bf16),
            vmem(chunks, bf16), vmem(chunks, bf16),
            vmem(chunks, bf16), vmem(chunks, bf16),
            vmem(chunks, bf16), vmem(chunks, bf16),
            vmem(chunks, f32),
            vmem((feats, feats // 2), f32),
            vmem((feats, feats // 2), bf16),
            dma((unembedding.shape[0] // DEPTH,)), dma((2, 16)), dma((2, 16)), dma,
            dma((n_chunk,)), dma((n_chunk,)), dma((n_chunk,)), dma((n_chunk,)),
            dma((2, UNITS)), dma((8, UNITS)), dma((2, 4, UNITS)),
            dma((2, n_chunk)), dma((2, n_chunk)), dma((2, n_chunk)),
            dma((2, n_chunk)), dma((2, n_chunk)), dma((2, n_chunk)),
            dma, dma, dma((3, 2)), dma((3, 2)), dma((8,)), dma((8,)), dma, dma, dma,
        ],
        compiler_params=pltpu.CompilerParams(
            collective_id=0, has_side_effects=True, vmem_limit_bytes=60 * 1024 * 1024
        ),
    )(row_ids, slots, expected, extra, unembedding, down_weight)
    return hidden_grad, (own + other.astype(f32)) / total_tokens


def shards(expected, labels, unembedding, down_weight):
    tokens = expected.shape[0]
    voc_shard = unembedding.shape[0]
    place = lax.axis_index("dp") * lax.axis_size("col") + lax.axis_index("col")
    ids = labels.reshape(-1, tokens)
    owner = ids // voc_shard
    before = lax.broadcasted_iota(jnp.int32, (1, tokens, tokens), 1) > lax.broadcasted_iota(
        jnp.int32, (1, tokens, tokens), 2
    )
    same_label = ids[:, :, None] == ids[:, None, :]
    is_first = jnp.logical_not(jnp.any(same_label & before, axis=2))
    ahead = (owner[:, :, None] == owner[:, None, :]) & before & is_first[:, None, :]
    rank = jnp.sum(ahead.astype(jnp.int32), axis=2)
    fits = jnp.max(jnp.where(is_first, rank, 0)) < CAP
    at_slot = ((owner == place) & is_first)[:, None, :] & (
        rank[:, None, :] == lax.broadcasted_iota(jnp.int32, (1, CAP, 1), 1)
    )
    row_ids = jnp.sum(jnp.where(at_slot, (ids - place * voc_shard)[:, None, :], 0), axis=2).reshape(1, -1)

    def mine(x):
        return lax.dynamic_slice_in_dim(x, place, 1, 0)

    own_ids = mine(ids)
    holds = (own_ids.reshape(tokens, 1) == own_ids) & mine(is_first).reshape(tokens, 1)
    slots = jnp.sum(jnp.where(holds, mine(owner * CAP + rank).reshape(tokens, 1), 0), axis=0, keepdims=True)
    extra = lax.cond(
        fits,
        lambda: jnp.zeros_like(expected),
        lambda: dense_rows(ids, unembedding, place),
    )
    slots = jnp.where(fits, slots, -1)
    return fast_shards(expected, extra, row_ids, slots, unembedding, down_weight)


def solution(mesh):
    in_specs = (P(("dp", "col"), "row"), P(), P(("dp", "col"), "row"), P("col", "row"))
    out_specs = (P(("dp", "row"), "col"), P("row", ("dp", "col")))
    return jax.shard_map(shards, mesh=mesh, in_specs=in_specs, out_specs=out_specs, check_vma=False)
```
